32 devices in a mesh: row: 16 (over z, y, x), col: 2 (over core).
Axes of the slice: x: 2, y: 2, z: 4, core: 2. Of those that a mesh axis runs over, the one named last changes fastest.
Arguments:
- root_cov: float32 [6144, 6144], P('row', 'col'), as said below
- structure: int32 [16], replicated, may hold values from 0 to 47, as said below
- child_factor: float32 [2048, 4096], P('row', 'col'), may hold values from -0.9 to 0.9
- child_diag: float32 [4096, 4096], P('row', 'col'), may hold values from -6 to 6
Outputs:
- cross_cov: float32 [2048, 4096], P('row', 'col')
- child_cov: float32 [4096, 4096], P('row', 'col')
The draws below stay inside these ranges and needn't reach their ends.
Inputs may be any that keep to these rules, and one draw needn't show every extreme that they name: root_cov is exactly symmetric and positive definite; its off-diagonal entries are small against its diagonal, which is about 1.5 times the product of a row scale and a column scale. `structure`: 16 distinct tiles in increasing order; the first and the last tile of the root are always among them, and so is tile R // 256 + 2 * R // 2048, which is the third tile of the list.
All inputs are finite; a program needn't handle non-finite values.
Results may differ from the reference program's by a relative error of at most 0.000078.
Values sent between devices are 32-bit elements; how exact they have to be, the bound alone decides.
A program may use at most 128 MiB of HBM per device.

```python
import math
import jax
import jax.numpy as jnp
from jax import lax

R = 6144
C = 4096
BLK = 128
KB = 16
K = 2048


def draw_root_cov(key, part):
    key_base = jax.random.fold_in(key, 11)
    base_draw = jax.random.normal(key_base, (R, R), jnp.float32)
    symmetric = (base_draw + base_draw.T) * (0.5 / math.sqrt(R))
    diagonal_mask = lax.iota(jnp.int32, R)[:, None] == lax.iota(jnp.int32, R)[None, :]
    core_matrix = jnp.where(diagonal_mask, 1.5, symmetric)
    return core_matrix.astype(jnp.float32)


def draw_structure(key, part):
    tile_count = R // BLK
    key_tile = tile_count // 2 + 2 * tile_count // KB
    lower_tile = jax.random.randint(jax.random.fold_in(key, 21), (1,), 1, key_tile).astype(jnp.int32)
    upper_pool = jax.random.permutation(jax.random.fold_in(key, 22), tile_count - key_tile - 2) + key_tile + 1
    upper_tiles = jnp.sort(upper_pool[:KB - 4]).astype(jnp.int32)
    first_tile = jnp.zeros((1,), jnp.int32)
    middle_tile = jnp.full((1,), key_tile, jnp.int32)
    last_tile = jnp.full((1,), tile_count - 1, jnp.int32)
    return jnp.concatenate([first_tile, lower_tile, middle_tile, upper_tiles, last_tile]).astype(jnp.int32)


def block_scale(own_key, dims, cuts, least, top_value):
    loudness, own = 1.0, jax.random.fold_in(own_key, 6)
    for axis_at, blocks in cuts:
        steps = jnp.exp(jax.random.uniform(jax.random.fold_in(own, axis_at), (blocks,), jnp.float32, least / len(cuts), top_value / len(cuts)))
        loudness = loudness * jnp.repeat(steps, dims[axis_at] // blocks).reshape([-1 if axis == axis_at else 1 for axis in range(len(dims))])
    return loudness


def gaussian(key, extent, scale, most, shards=(), kind=jnp.bfloat16):
    array = jax.random.normal(key, extent, jnp.float32) * scale
    if len(shards) > 0:
        array = block_scale(key, extent, shards, -0.22, 0.18) * array
    return jnp.clip(array, min=-most, max=most).astype(kind)


def setup_inputs(seed: int = 0) -> dict:
    key_list = jax.random.split(jax.random.key(seed), 5)
    root_cov = draw_root_cov(jax.random.fold_in(key_list[4], 71), 0)
    structure = draw_structure(jax.random.fold_in(key_list[4], 71), 0)
    child_factor = gaussian(key_list[2], (K, C), 0.15, 0.9, ((0, 16), (1, 2)), jnp.float32)
    child_diag = gaussian(key_list[3], (C, C), 1.0, 6.0, ((0, 16), (1, 2)), jnp.float32)
    return {"root_cov": root_cov, "structure": structure, "child_factor": child_factor, "child_diag": child_diag}


def reference(root_cov, structure, child_factor, child_diag):
    offsets = jnp.arange(BLK, dtype=jnp.int32)
    struct_rows = (structure[:, None] * BLK + offsets[None, :]).reshape(-1).astype(jnp.int32)
    selected = jnp.take(jnp.take(root_cov, struct_rows, axis=0), struct_rows, axis=1)
    cross_cov = -jnp.dot(selected, child_factor, precision=lax.Precision.HIGHEST, preferred_element_type=jnp.float32)
    product = jnp.dot(child_factor.T, cross_cov, precision=lax.Precision.HIGHEST, preferred_element_type=jnp.float32)
    child_cov = child_diag - product
    return (cross_cov, child_cov)
```

```python
import jax
import jax.numpy as jnp
from jax import lax
from jax.sharding import Mesh, PartitionSpec as P

BLK = 128
NB = 4
HIGH = lax.Precision.HIGH


def contract_rows(first_mat, second_mat):
    return lax.dot_general(
        first_mat,
        second_mat,
        (((0,), (0,)), ((), ())),
        precision=HIGH,
        preferred_element_type=jnp.float32,
    )


def plain_device(root_cov, structure, child_factor, child_diag):
    rows_dev = root_cov.shape[0]
    offsets = lax.iota(jnp.int32, BLK)
    struct_rows = (structure[:, None] * BLK + offsets[None, :]).reshape(-1)
    row_index = lax.axis_index("row")
    global_rows = row_index * rows_dev + lax.iota(jnp.int32, rows_dev)
    tile_index = global_rows // BLK
    rank_count = jnp.sum((structure[None, :] < tile_index[:, None]).astype(jnp.int32), axis=1)
    member = jnp.any(structure[None, :] == tile_index[:, None], axis=1)
    position = rank_count * BLK + global_rows % BLK
    picked = jnp.take(lax.all_gather(root_cov, "col", axis=1, tiled=True), struct_rows, axis=1)
    factor = lax.all_gather(child_factor, "row", axis=0, tiled=True)
    rows = jnp.take(factor, jnp.clip(position, 0, factor.shape[0] - 1), axis=0)
    spread = jnp.where(member[:, None], rows, 0.0)
    cross_cov = lax.psum_scatter(
        -contract_rows(picked, spread), "row", scatter_dimension=0, tiled=True
    )
    factor_rows = lax.all_gather(child_factor, "col", axis=1, tiled=True)
    child_cov = child_diag + lax.psum_scatter(
        -contract_rows(factor_rows, cross_cov), "row", scatter_dimension=0, tiled=True
    )
    return (cross_cov, child_cov)


def select_quarter(root_cov, structure, z, b, c):
    tiles_dev = root_cov.shape[0] // BLK
    col_tiles = root_cov.shape[1] // BLK
    kb = structure.shape[0]
    parts = []
    for j in range(kb):
        at = structure[j] - c * col_tiles
        inside = (at >= 0) & (at < col_tiles)
        start = jnp.clip(at, 0, col_tiles - 1) * BLK
        piece = lax.dynamic_slice(root_cov, (0, start), (root_cov.shape[0], BLK))
        parts.append(jnp.where(inside, piece, 0.0))
    picked = jnp.concatenate(parts, axis=1)
    half = lax.psum_scatter(picked, "col", scatter_dimension=1, tiled=True)
    first = (z * NB + b) * tiles_dev
    parts = []
    for j in range(kb):
        at = structure[j] - first
        inside = (at >= 0) & (at < tiles_dev)
        start = jnp.clip(at, 0, tiles_dev - 1) * BLK
        piece = lax.dynamic_slice(half, (start, 0), (BLK, half.shape[1]))
        parts.append(jnp.where(inside, piece, 0.0))
    full = jnp.concatenate(parts, axis=0)
    mine = lax.psum_scatter(full, ("z", "b"), scatter_dimension=0, tiled=True)
    quarter = lax.all_gather(mine, "z", axis=0, tiled=True)
    return lax.all_gather(quarter, "col", axis=1, tiled=True)


def grouped_device(root_cov, structure, child_factor, child_diag):
    z, b, c = lax.axis_index("z"), lax.axis_index("b"), lax.axis_index("col")
    nz = lax.axis_size("z")
    depth, width = child_factor.shape
    k = depth * nz * NB
    zh = nz // 2
    sub = width // (zh * NB)
    f4 = child_factor.reshape(depth, zh, NB, sub)
    f_i = lax.all_to_all(f4, "b", split_axis=2, concat_axis=0, tiled=True)
    f_i = lax.all_gather(f_i.reshape(NB * depth, zh * sub), "z", axis=0, tiled=True)
    quarter = select_quarter(root_cov, structure, z, b, c)
    own = lax.dynamic_slice(f_i, (0, (z % zh) * sub), (k, sub))
    other = lax.ppermute(own, "col", [(0, 1), (1, 0)])
    own = jnp.where(c == z // zh, own, other)
    hs = sub // 2
    own = lax.dynamic_slice(own, (0, c * hs), (k, hs))
    f_j = lax.all_gather(own, "b", axis=1, tiled=True)
    x = -jnp.dot(quarter, f_j, precision=HIGH, preferred_element_type=jnp.float32)
    x3 = x.reshape(nz, depth, NB * hs)
    x_all = lax.all_gather(x3, "b", axis=1, tiled=False).reshape(k, NB * hs)
    x_all = lax.all_gather(x_all, "col", axis=0, tiled=False)
    out = lax.dot_general(
        x_all, f_i, (((1,), (0,)), ((), ())), precision=HIGH,
        preferred_element_type=jnp.float32,
    )
    out = out.reshape(2, NB, hs, zh * sub)
    out = lax.all_to_all(out, "b", split_axis=1, concat_axis=1, tiled=True)
    out = out.reshape(2, NB, hs, zh, sub).transpose(0, 2, 3, 1, 4).reshape(2 * hs, width)
    child_cov = child_diag - out
    y = lax.all_to_all(x3, "z", split_axis=0, concat_axis=0, tiled=True)
    y = y.reshape(2, zh, depth, NB, hs)
    y = lax.all_to_all(y, "col", split_axis=0, concat_axis=0, tiled=True)
    cross_cov = y.transpose(2, 1, 3, 0, 4).reshape(depth, width)
    return (cross_cov, child_cov)


def solution(mesh):
    rows, cols = mesh.shape["row"], mesh.shape["col"]
    if cols == 2 and rows == 4 * NB:
        split = Mesh(mesh.devices.reshape(rows // NB, NB, cols), ("z", "b", "col"))
        spec = P(("z", "b"), "col")
        return jax.shard_map(
            grouped_device, mesh=split, in_specs=(spec, P(), spec, spec),
            out_specs=(spec, spec), check_vma=False,
        )
    spec = P("row", "col")
    return jax.shard_map(
        plain_device, mesh=mesh, in_specs=(spec, P(), spec, spec),
        out_specs=(spec, spec), check_vma=False,
    )
```

```python
import jax
import jax.numpy as jnp
from jax import lax
from jax.experimental import pallas as pl
from jax.experimental.pallas import tpu as pltpu
from jax.sharding import Mesh, PartitionSpec as P

BLK = 128
NB = 4
HIGH = lax.Precision.HIGH
MESH = pl.DeviceIdType.MESH


def contract_rows(first_mat, second_mat):
    return lax.dot_general(
        first_mat,
        second_mat,
        (((0,), (0,)), ((), ())),
        precision=HIGH,
        preferred_element_type=jnp.float32,
    )


def plain_device(root_cov, structure, child_factor, child_diag):
    rows_dev = root_cov.shape[0]
    offsets = lax.iota(jnp.int32, BLK)
    struct_rows = (structure[:, None] * BLK + offsets[None, :]).reshape(-1)
    row_index = lax.axis_index("row")
    global_rows = row_index * rows_dev + lax.iota(jnp.int32, rows_dev)
    tile_index = global_rows // BLK
    rank_count = jnp.sum((structure[None, :] < tile_index[:, None]).astype(jnp.int32), axis=1)
    member = jnp.any(structure[None, :] == tile_index[:, None], axis=1)
    position = rank_count * BLK + global_rows % BLK
    picked = jnp.take(lax.all_gather(root_cov, "col", axis=1, tiled=True), struct_rows, axis=1)
    factor = lax.all_gather(child_factor, "row", axis=0, tiled=True)
    rows = jnp.take(factor, jnp.clip(position, 0, factor.shape[0] - 1), axis=0)
    spread = jnp.where(member[:, None], rows, 0.0)
    cross_cov = lax.psum_scatter(
        -contract_rows(picked, spread), "row", scatter_dimension=0, tiled=True
    )
    factor_rows = lax.all_gather(child_factor, "col", axis=1, tiled=True)
    child_cov = child_diag + lax.psum_scatter(
        -contract_rows(factor_rows, cross_cov), "row", scatter_dimension=0, tiled=True
    )
    return (cross_cov, child_cov)


def gather_kernel(f_ref, a_ref, fi, fj, s, slo, loc, ssem, rp, rplane, rj, rs, rsib, rlo):
    z, b, c = lax.axis_index("z"), lax.axis_index("b"), lax.axis_index("col")
    low, high = z > 0, z < 3
    home = c == z // 2
    peers = [lax.rem(b + d, NB) for d in range(NB)]
    sources = [lax.rem(b + NB - d, NB) for d in range(NB)]

    barrier = pltpu.get_barrier_semaphore()

    def greet(zz, bb, cc):
        pl.semaphore_signal(
            barrier, inc=1, device_id={"z": zz, "b": bb, "col": cc}, device_id_type=MESH
        )

    for d in range(NB):
        if d:
            greet(z, peers[d], c)
        greet(z, peers[d], 1 - c)
    pl.when(low)(lambda: greet(z - 1, b, c))
    pl.when(high)(lambda: greet(z + 1, b, c))
    pl.semaphore_wait(barrier, 2 * NB - 1 + low.astype(jnp.int32) + high.astype(jnp.int32))

    sent = []

    def send(cond, src, dst, rsem, zz, bb, cc):
        at = len(sent)
        copy = lambda: pltpu.make_async_remote_copy(
            src_ref=src(), dst_ref=dst(), send_sem=ssem.at[at], recv_sem=rsem(),
            device_id={"z": zz, "b": bb, "col": cc}, device_id_type=MESH,
        )
        sent.append((cond, copy))
        pl.when(cond)(lambda: copy().start())

    def arrived(cond, ref, sem):
        @pl.when(cond)
        def _():
            pltpu.make_async_copy(ref(), ref(), sem()).wait()

    always = z >= 0
    for t in range(2):
        own = z == t + 2
        send(own, lambda: a_ref, lambda t=t: s.at[t, c], lambda t=t: rs.at[t], z - 1, b, c)
        if t == 0:
            send(own, lambda: a_ref, lambda: s.at[0, c], lambda: rs.at[0], z + 1, b, c)

        @pl.when(own)
        def _(t=t):
            pltpu.make_async_copy(a_ref, s.at[t, c], loc.at[0]).start()
    for d in range(1, NB):
        send(always, lambda d=d: f_ref.at[peers[d]], lambda: fi.at[NB * z + b],
             lambda d=d: rplane.at[d], z, peers[d], c)
    mine = pltpu.make_async_copy(f_ref.at[b], fi.at[NB * z + b], loc.at[1])
    mine.start()
    mine.wait()

    off = lax.rem(z, 2) * 256

    def rows(zz):
        return pl.ds(NB * zz, NB)

    def piece(zz, cc):
        lanes = pl.ds(pl.multiple_of(off + 128 * cc, 128), 128)
        return fi.at[rows(zz), :, lanes]

    def slot(zz, bb):
        return fj.at[rows(zz), :, pl.ds(pl.multiple_of(bb * 128, 128), 128)]

    def spread_plane(cond, zz, h):
        take = jnp.logical_and(cond, home)
        for d in range(NB):
            for other in range(2):
                cc = 1 - c if other else c
                if d == 0 and not other:
                    @pl.when(take)
                    def _():
                        pltpu.make_async_copy(piece(zz, cc), slot(zz, b), loc.at[2 + h]).start()
                else:
                    send(take, lambda cc=cc: piece(zz, cc), lambda: slot(zz, b),
                         lambda: rj.at[b * NB + zz], z, peers[d], cc)

    def spread_rows(cond, t):
        send(cond, lambda: s.at[t, c], lambda: s.at[t, c], lambda: rsib.at[t], z, b, 1 - c)
        take = jnp.logical_and(cond, c == 0)
        low_cols = lambda: s.at[t, 0, :, :, pl.ds(0, 256)]
        for d in range(1, NB):
            for cc in range(2):
                send(take, low_cols, lambda: slo.at[b, t], lambda: rlo.at[b * 2 + t], z, peers[d], cc)

    for d in range(1, NB):
        arrived(always, lambda d=d: fi.at[NB * z + sources[d]], lambda d=d: rplane.at[d])
    plane = lambda zz: (lambda: fi.at[rows(zz)])
    send(high, plane(z), plane(z), lambda: rp.at[z], z + 1, b, c)
    send(low, plane(z), plane(z), lambda: rp.at[z], z - 1, b, c)
    spread_plane(always, z, 0)
    for t in range(2):
        own = z == t + 2

        @pl.when(own)
        def _(t=t):
            pltpu.make_async_copy(a_ref, s.at[t, c], loc.at[0]).wait()
        spread_rows(own, t)
    slots = 2
    for h in range(1, 4):
        for up in (False, True):
            zz = z - h if up else z + h
            here = zz >= 0 if up else zz <= 3
            on = jnp.logical_and(here, high if up else low)
            nxt = z + 1 if up else z - 1
            for t in range(2):
                got = jnp.logical_and(here, zz == t + 2)
                if up and (t == 1 or h > 1):
                    continue
                arrived(got, lambda t=t: s.at[t, c], lambda t=t: rs.at[t])
                if not up:
                    send(jnp.logical_and(got, low), lambda t=t: s.at[t, c], lambda t=t: s.at[t, c],
                         lambda t=t: rs.at[t], nxt, b, c)
                spread_rows(got, t)
            arrived(here, plane(zz), lambda zz=zz: rp.at[zz])
            send(on, plane(zz), plane(zz), lambda zz=zz: rp.at[zz], nxt, b, c)
            spread_plane(here, zz, 2 * h - 1 + int(up))
    for t in range(2):
        arrived(always, lambda t=t: s.at[t, 1 - c], lambda t=t: rsib.at[t])
        for d in range(1, NB):
            arrived(always, lambda d=d, t=t: slo.at[peers[d], t],
                    lambda d=d, t=t: rlo.at[peers[d] * 2 + t])
    for zz in range(4):
        for d in range(NB):
            cond = always if d else jnp.logical_not(home)
            arrived(cond, lambda zz=zz, d=d: slot(zz, peers[d]),
                    lambda zz=zz, d=d: rj.at[peers[d] * NB + zz])
    for h in range(4):
        for up in (False, True):
            if h == 0 and up:
                continue
            zz = z if h == 0 else (z - h if up else z + h)
            here = jnp.logical_and(zz >= 0, zz <= 3)

            @pl.when(jnp.logical_and(here, home))
            def _(zz=zz, h=h, up=up):
                sem = loc.at[2 + (2 * h - 1 + int(up) if h else 0)]
                pltpu.make_async_copy(piece(zz, c), slot(zz, b), sem).wait()
    for cond, copy in sent:
        pl.when(cond)(lambda: copy().wait_send())


def gather_blocks(f_b, a):
    any_spec = pl.BlockSpec(memory_space=pl.ANY)
    f32 = jnp.float32
    dma = pltpu.SemaphoreType.DMA
    return pl.pallas_call(
        gather_kernel,
        out_shape=(
            jax.ShapeDtypeStruct((16, BLK, 512), f32),
            jax.ShapeDtypeStruct((16, BLK, 512), f32),
            jax.ShapeDtypeStruct((2, 2, 3, BLK, 1024), f32),
            jax.ShapeDtypeStruct((NB, 2, 3, BLK, 256), f32),
        ),
        in_specs=[any_spec] * 2,
        out_specs=(any_spec,) * 4,
        scratch_shapes=[
            dma((9,)), dma((160,)), dma((4,)), dma((NB,)), dma((16,)), dma((2,)), dma((2,)), dma((8,)),
        ],
        compiler_params=pltpu.CompilerParams(collective_id=0, has_side_effects=True),
        name="gather_blocks",
    )(f_b, a)


def grouped_device(root_cov, structure, child_factor, child_diag):
    z, b, c = lax.axis_index("z"), lax.axis_index("b"), lax.axis_index("col")
    nz = lax.axis_size("z")
    depth, width = child_factor.shape
    k = depth * nz * NB
    zh = nz // 2
    sub = width // (zh * NB)
    hs = sub // 2
    tiles_dev = root_cov.shape[0] // BLK
    col_tiles = root_cov.shape[1] // BLK
    kb = structure.shape[0]
    parts = []
    for j in range(kb):
        at = structure[j] - c * col_tiles
        inside = (at >= 0) & (at < col_tiles)
        start = jnp.clip(at, 0, col_tiles - 1) * BLK
        piece = lax.dynamic_slice(root_cov, (0, start), (root_cov.shape[0], BLK))
        parts.append(jnp.where(inside, piece, 0.0))
    picked = jnp.concatenate(parts, axis=1)
    half = lax.psum_scatter(picked, "col", scatter_dimension=1, tiled=True)
    first = (z * NB + b) * tiles_dev
    parts = []
    for j in range(2):
        at = structure[j] - first
        inside = (at >= 0) & (at < tiles_dev) & (c == 0)
        start = jnp.clip(at, 0, tiles_dev - 1) * BLK
        piece = lax.dynamic_slice(half, (start, 0), (BLK, 2 * BLK))
        parts.append(jnp.where(inside, piece, 0.0))
    low_low = lax.psum(jnp.concatenate(parts, axis=0), ("z", "b", "col"))
    f_b = child_factor.reshape(depth, zh, NB, sub).transpose(2, 0, 1, 3).reshape(NB, depth, zh * sub)
    f_i, f_j, s, slo = gather_blocks(f_b, half.reshape(tiles_dev, BLK, half.shape[1]))
    f_i = f_i.reshape(k, zh * sub)
    f_j = f_j.reshape(k, NB * hs)
    rows = s.transpose(0, 2, 3, 1, 4).reshape(2 * tiles_dev, BLK, k)
    place = (structure // 3) % NB * 6 + (structure // 12 - 2) * 3 + structure % 3
    low_own = s[:, 0, :, :, : 2 * BLK]
    low_all = jnp.where((lax.iota(jnp.int32, NB) == b)[:, None, None, None, None], low_own[None], slo)
    col = jnp.minimum(b, 1) * BLK
    low_all = lax.dynamic_slice_in_dim(low_all.reshape(NB * 6, BLK, 2 * BLK), col, BLK, axis=2)
    low_row = jnp.take(low_all, place[2:], axis=0, mode="clip").reshape((kb - 2) * BLK, BLK).T
    low_row = jnp.concatenate([lax.dynamic_slice(low_low, (col, 0), (BLK, 2 * BLK)), low_row], axis=1)
    spare = jnp.where(b < 2, low_row, rows[0])
    rows = jnp.concatenate([spare[None], rows[1:]], axis=0).reshape(6 * BLK, k)
    x = -jnp.dot(rows, f_j, precision=HIGH, preferred_element_type=jnp.float32)
    x_all = lax.all_gather(x, "b", axis=0, tiled=True).reshape(NB * 6, BLK, NB * hs)
    place = jnp.concatenate([jnp.array([0, 6], jnp.int32), place[2:]])
    x_all = jnp.concatenate(
        [lax.dynamic_slice_in_dim(x_all, place[j], 1, axis=0) for j in range(kb)], axis=0)
    x3 = lax.dynamic_slice_in_dim(x_all.reshape(nz, NB, depth, NB * hs), b, 1, axis=1)[:, 0]
    x_all = lax.all_gather(x_all.reshape(k, NB * hs), "col", axis=0, tiled=False)
    out = lax.dot_general(
        x_all, f_i, (((1,), (0,)), ((), ())), precision=HIGH,
        preferred_element_type=jnp.float32,
    )
    out = out.reshape(2, NB, hs, zh * sub)
    out = lax.all_to_all(out, "b", split_axis=1, concat_axis=1, tiled=True)
    out = out.reshape(2, NB, hs, zh, sub).transpose(0, 2, 3, 1, 4).reshape(2 * hs, width)
    child_cov = child_diag - out
    y = lax.all_to_all(x3, "z", split_axis=0, concat_axis=0, tiled=True)
    y = y.reshape(2, zh, depth, NB, hs)
    y = lax.all_to_all(y, "col", split_axis=0, concat_axis=0, tiled=True)
    cross_cov = y.transpose(2, 1, 3, 0, 4).reshape(depth, width)
    return (cross_cov, child_cov)


def solution(mesh):
    rows, cols = mesh.shape["row"], mesh.shape["col"]
    if cols == 2 and rows == 4 * NB:
        split = Mesh(mesh.devices.reshape(rows // NB, NB, cols), ("z", "b", "col"))
        spec = P(("z", "b"), "col")
        return jax.shard_map(
            grouped_device, mesh=split, in_specs=(spec, P(), spec, spec),
            out_specs=(spec, spec), check_vma=False,
        )
    spec = P("row", "col")
    return jax.shard_map(
        plain_device, mesh=mesh, in_specs=(spec, P(), spec, spec),
        out_specs=(spec, spec), check_vma=False,
    )
```

```python
import jax
import jax.numpy as jnp
from jax import lax
from jax.experimental import pallas as pl
from jax.experimental.pallas import tpu as pltpu
from jax.sharding import Mesh, PartitionSpec as P

BLK = 128
NB = 4
HIGH = lax.Precision.HIGH
MESH = pl.DeviceIdType.MESH


def contract_rows(first_mat, second_mat):
    return lax.dot_general(
        first_mat,
        second_mat,
        (((0,), (0,)), ((), ())),
        precision=HIGH,
        preferred_element_type=jnp.float32,
    )


def plain_device(root_cov, structure, child_factor, child_diag):
    rows_dev = root_cov.shape[0]
    offsets = lax.iota(jnp.int32, BLK)
    struct_rows = (structure[:, None] * BLK + offsets[None, :]).reshape(-1)
    row_index = lax.axis_index("row")
    global_rows = row_index * rows_dev + lax.iota(jnp.int32, rows_dev)
    tile_index = global_rows // BLK
    rank_count = jnp.sum((structure[None, :] < tile_index[:, None]).astype(jnp.int32), axis=1)
    member = jnp.any(structure[None, :] == tile_index[:, None], axis=1)
    position = rank_count * BLK + global_rows % BLK
    picked = jnp.take(lax.all_gather(root_cov, "col", axis=1, tiled=True), struct_rows, axis=1)
    factor = lax.all_gather(child_factor, "row", axis=0, tiled=True)
    rows = jnp.take(factor, jnp.clip(position, 0, factor.shape[0] - 1), axis=0)
    spread = jnp.where(member[:, None], rows, 0.0)
    cross_cov = lax.psum_scatter(
        -contract_rows(picked, spread), "row", scatter_dimension=0, tiled=True
    )
    factor_rows = lax.all_gather(child_factor, "col", axis=1, tiled=True)
    child_cov = child_diag + lax.psum_scatter(
        -contract_rows(factor_rows, cross_cov), "row", scatter_dimension=0, tiled=True
    )
    return (cross_cov, child_cov)


def select_kernel(at_ref, inside_ref, x_ref, o_ref):
    o_ref[...] = jnp.where(inside_ref[pl.program_id(0)] > 0, x_ref[...], 0.0)


def select_columns(mat, tiles):
    rows, cols = mat.shape
    inside = ((tiles >= 0) & (tiles < cols // BLK)).astype(jnp.int32)
    kb = tiles.shape[0]
    return pl.pallas_call(
        select_kernel,
        out_shape=jax.ShapeDtypeStruct((rows, kb * BLK), mat.dtype),
        grid_spec=pltpu.PrefetchScalarGridSpec(
            num_scalar_prefetch=2, grid=(kb,),
            in_specs=[pl.BlockSpec((rows, BLK), lambda j, at, ok: (0, at[j]))],
            out_specs=pl.BlockSpec((rows, BLK), lambda j, at, ok: (0, j)),
        ),
        name="select_columns",
    )(jnp.clip(tiles, 0, cols // BLK - 1), inside, mat)


def permute_kernel(at_ref, x_ref, o_ref):
    o_ref[...] = x_ref[...]


def permute_tiles(x, place):
    _, depth, width = x.shape
    kb = place.shape[0]
    return pl.pallas_call(
        permute_kernel,
        out_shape=jax.ShapeDtypeStruct((kb, depth, width), x.dtype),
        grid_spec=pltpu.PrefetchScalarGridSpec(
            num_scalar_prefetch=1, grid=(kb,),
            in_specs=[pl.BlockSpec((1, depth, width), lambda j, at: (at[j], 0, 0))],
            out_specs=pl.BlockSpec((1, depth, width), lambda j, at: (j, 0, 0)),
        ),
        name="permute_tiles",
    )(place, x)


def scatter_kernel(o_ref, x_ref, res, y, loc, ssem, rres, ry):
    z, b, c = lax.axis_index("z"), lax.axis_index("b"), lax.axis_index("col")
    home = c == z // 2
    away = jnp.logical_not(home)
    peers = [lax.rem(b + d, NB) for d in range(NB)]
    sources = [lax.rem(b + NB - d, NB) for d in range(NB)]
    planes = [lax.rem(z + d, 4) for d in range(4)]
    barrier = pltpu.get_barrier_semaphore()

    def greet(zz, bb, cc):
        pl.semaphore_signal(
            barrier, inc=1, device_id={"z": zz, "b": bb, "col": cc}, device_id_type=MESH
        )

    for d in range(1, NB):
        greet(z, peers[d], c)
        greet(planes[d], b, c)
    for d in range(4):
        greet(planes[d], b, 1 - c)
    pl.semaphore_wait(barrier, 10)

    def block(bb, zi):
        return pl.ds(pl.multiple_of(zi * 1024 + bb * 256, 128), 256)

    def lanes(zi, bb, cc):
        return pl.ds(pl.multiple_of(zi * 1024 + bb * 256 + cc * 128, 128), 128)

    always = z >= 0
    sent, local = [], []

    def send(cond, src, dst, rsem, zz, bb, cc):
        copy = pltpu.make_async_remote_copy(
            src_ref=src, dst_ref=dst, send_sem=ssem.at[len(sent)], recv_sem=rsem,
            device_id={"z": zz, "b": bb, "col": cc}, device_id_type=MESH,
        )
        sent.append((cond, copy))
        pl.when(cond)(lambda: copy.start())

    def keep(cond, src, dst):
        copy = pltpu.make_async_copy(src, dst, loc.at[len(local)])
        local.append((cond, copy))
        pl.when(cond)(lambda: copy.start())

    for d in range(1, NB):
        for q in range(2):
            for zi in range(2):
                send(always, o_ref.at[q, peers[d], :, pl.ds(zi * 256, 256)], res.at[q, :, block(b, zi)],
                     rres.at[4 * d + 2 * q + zi], z, peers[d], c)
    zpar = lax.rem(z, 2)
    for d in range(4):
        for bb in range(NB):
            src = x_ref.at[planes[d], :, pl.ds(bb * 128, 128)]
            dst = y.at[:, lanes(zpar, bb, c)]
            if d == 0:
                keep(home, src, dst)
                send(away, src, dst, ry.at[(2 * z + c) * NB + bb], z, b, 1 - c)
            else:
                send(always, src, dst, ry.at[(2 * z + c) * NB + bb], planes[d], b, z // 2)
    for q in range(2):
        for zi in range(2):
            keep(always, o_ref.at[q, b, :, pl.ds(zi * 256, 256)], res.at[q, :, block(b, zi)])

    for d in range(1, NB):
        for q in range(2):
            for zi in range(2):
                ref = res.at[q, :, block(sources[d], zi)]
                pltpu.make_async_copy(ref, ref, rres.at[4 * d + 2 * q + zi]).wait()
    for zi in range(2):
        for cc in range(2):
            zz = 2 * c + zi
            other = jnp.logical_or(zz != z, c != cc)
            for bb in range(NB):
                ref = y.at[:, lanes(zi, bb, cc)]
                copy = pltpu.make_async_copy(ref, ref, ry.at[(2 * zz + cc) * NB + bb])
                pl.when(other)(lambda copy=copy: copy.wait())
    for cond, copy in local:
        pl.when(cond)(lambda copy=copy: copy.wait())
    for cond, copy in sent:
        pl.when(cond)(lambda copy=copy: copy.wait_send())


def scatter_blocks(out, x3):
    any_spec = pl.BlockSpec(memory_space=pl.ANY)
    dma = pltpu.SemaphoreType.DMA
    return pl.pallas_call(
        scatter_kernel,
        out_shape=(
            jax.ShapeDtypeStruct((2, BLK, 2048), jnp.float32),
            jax.ShapeDtypeStruct((BLK, 2048), jnp.float32),
        ),
        in_specs=[any_spec] * 2,
        out_specs=(any_spec,) * 2,
        scratch_shapes=[dma((8,)), dma((28,)), dma((16,)), dma((32,))],
        compiler_params=pltpu.CompilerParams(collective_id=1, has_side_effects=True),
        name="scatter_blocks",
    )(out, x3)


def gather_kernel(f_ref, a_ref, fi, fj, s, slo, loc, ssem, rp, rplane, rj, rs, rsib, rlo):
    z, b, c = lax.axis_index("z"), lax.axis_index("b"), lax.axis_index("col")
    low, high = z > 0, z < 3
    home = c == z // 2
    peers = [lax.rem(b + d, NB) for d in range(NB)]
    sources = [lax.rem(b + NB - d, NB) for d in range(NB)]

    barrier = pltpu.get_barrier_semaphore()

    def greet(zz, bb, cc):
        pl.semaphore_signal(
            barrier, inc=1, device_id={"z": zz, "b": bb, "col": cc}, device_id_type=MESH
        )

    for d in range(NB):
        if d:
            greet(z, peers[d], c)
        greet(z, peers[d], 1 - c)
    pl.when(low)(lambda: greet(z - 1, b, c))
    pl.when(high)(lambda: greet(z + 1, b, c))
    pl.semaphore_wait(barrier, 2 * NB - 1 + low.astype(jnp.int32) + high.astype(jnp.int32))

    sent = []

    def rows_half(t, cc):
        return s.at[t, :, :, pl.ds(pl.multiple_of(cc * 1024, 128), 1024)]

    def send(cond, src, dst, rsem, zz, bb, cc):
        at = len(sent)
        copy = lambda: pltpu.make_async_remote_copy(
            src_ref=src(), dst_ref=dst(), send_sem=ssem.at[at], recv_sem=rsem(),
            device_id={"z": zz, "b": bb, "col": cc}, device_id_type=MESH,
        )
        sent.append((cond, copy))
        pl.when(cond)(lambda: copy().start())

    def arrived(cond, ref, sem):
        @pl.when(cond)
        def _():
            pltpu.make_async_copy(ref(), ref(), sem()).wait()

    always = z >= 0
    for t in range(2):
        own = z == t + 2
        send(own, lambda: a_ref, lambda t=t: rows_half(t, c), lambda t=t: rs.at[t], z - 1, b, c)
        if t == 0:
            send(own, lambda: a_ref, lambda: rows_half(0, c), lambda: rs.at[0], z + 1, b, c)

        @pl.when(own)
        def _(t=t):
            pltpu.make_async_copy(a_ref, rows_half(t, c), loc.at[0]).start()
    for d in range(1, NB):
        send(always, lambda d=d: f_ref.at[peers[d]], lambda: fi.at[NB * z + b],
             lambda d=d: rplane.at[d], z, peers[d], c)
    mine = pltpu.make_async_copy(f_ref.at[b], fi.at[NB * z + b], loc.at[1])
    mine.start()
    mine.wait()

    off = lax.rem(z, 2) * 256

    def rows(zz):
        return pl.ds(NB * zz, NB)

    def piece(zz, cc):
        lanes = pl.ds(pl.multiple_of(off + 128 * cc, 128), 128)
        return fi.at[rows(zz), :, lanes]

    def slot(zz, bb):
        return fj.at[rows(zz), :, pl.ds(pl.multiple_of(bb * 128, 128), 128)]

    def spread_plane(cond, zz, h):
        take = jnp.logical_and(cond, home)
        for d in range(NB):
            for other in range(2):
                cc = 1 - c if other else c
                if d == 0 and not other:
                    @pl.when(take)
                    def _():
                        pltpu.make_async_copy(piece(zz, cc), slot(zz, b), loc.at[2 + h]).start()
                else:
                    send(take, lambda cc=cc: piece(zz, cc), lambda: slot(zz, b),
                         lambda: rj.at[b * NB + zz], z, peers[d], cc)

    def spread_rows(cond, t):
        send(cond, lambda: rows_half(t, c), lambda: rows_half(t, c), lambda: rsib.at[t], z, b, 1 - c)
        take = jnp.logical_and(cond, c == 0)
        low_cols = lambda: s.at[t, :, :, pl.ds(0, 256)]
        for d in range(1, NB):
            for cc in range(2):
                send(take, low_cols, lambda: slo.at[b, t], lambda: rlo.at[b * 2 + t], z, peers[d], cc)

    for d in range(1, NB):
        arrived(always, lambda d=d: fi.at[NB * z + sources[d]], lambda d=d: rplane.at[d])
    plane = lambda zz: (lambda: fi.at[rows(zz)])
    send(high, plane(z), plane(z), lambda: rp.at[z], z + 1, b, c)
    send(low, plane(z), plane(z), lambda: rp.at[z], z - 1, b, c)
    spread_plane(always, z, 0)
    for t in range(2):
        own = z == t + 2

        @pl.when(own)
        def _(t=t):
            pltpu.make_async_copy(a_ref, rows_half(t, c), loc.at[0]).wait()
        spread_rows(own, t)
    slots = 2
    for h in range(1, 4):
        for up in (False, True):
            zz = z - h if up else z + h
            here = zz >= 0 if up else zz <= 3
            on = jnp.logical_and(here, high if up else low)
            nxt = z + 1 if up else z - 1
            for t in range(2):
                got = jnp.logical_and(here, zz == t + 2)
                if up and (t == 1 or h > 1):
                    continue
                arrived(got, lambda t=t: rows_half(t, c), lambda t=t: rs.at[t])
                if not up:
                    send(jnp.logical_and(got, low), lambda t=t: rows_half(t, c), lambda t=t: rows_half(t, c),
                         lambda t=t: rs.at[t], nxt, b, c)
                spread_rows(got, t)
            arrived(here, plane(zz), lambda zz=zz: rp.at[zz])
            send(on, plane(zz), plane(zz), lambda zz=zz: rp.at[zz], nxt, b, c)
            spread_plane(here, zz, 2 * h - 1 + int(up))
    for t in range(2):
        arrived(always, lambda t=t: rows_half(t, 1 - c), lambda t=t: rsib.at[t])
        for d in range(1, NB):
            arrived(always, lambda d=d, t=t: slo.at[peers[d], t],
                    lambda d=d, t=t: rlo.at[peers[d] * 2 + t])
    for zz in range(4):
        for d in range(NB):
            cond = always if d else jnp.logical_not(home)
            arrived(cond, lambda zz=zz, d=d: slot(zz, peers[d]),
                    lambda zz=zz, d=d: rj.at[peers[d] * NB + zz])
    for h in range(4):
        for up in (False, True):
            if h == 0 and up:
                continue
            zz = z if h == 0 else (z - h if up else z + h)
            here = jnp.logical_and(zz >= 0, zz <= 3)

            @pl.when(jnp.logical_and(here, home))
            def _(zz=zz, h=h, up=up):
                sem = loc.at[2 + (2 * h - 1 + int(up) if h else 0)]
                pltpu.make_async_copy(piece(zz, c), slot(zz, b), sem).wait()
    for cond, copy in sent:
        pl.when(cond)(lambda: copy().wait_send())


def gather_blocks(f_b, a):
    any_spec = pl.BlockSpec(memory_space=pl.ANY)
    f32 = jnp.float32
    dma = pltpu.SemaphoreType.DMA
    return pl.pallas_call(
        gather_kernel,
        out_shape=(
            jax.ShapeDtypeStruct((16, BLK, 512), f32),
            jax.ShapeDtypeStruct((16, BLK, 512), f32),
            jax.ShapeDtypeStruct((2, 3, BLK, 2048), f32),
            jax.ShapeDtypeStruct((NB, 2, 3, BLK, 256), f32),
        ),
        in_specs=[any_spec] * 2,
        out_specs=(any_spec,) * 4,
        scratch_shapes=[
            dma((9,)), dma((160,)), dma((4,)), dma((NB,)), dma((16,)), dma((2,)), dma((2,)), dma((8,)),
        ],
        compiler_params=pltpu.CompilerParams(collective_id=0, has_side_effects=True),
        name="gather_blocks",
    )(f_b, a)


def grouped_device(root_cov, structure, child_factor, child_diag):
    z, b, c = lax.axis_index("z"), lax.axis_index("b"), lax.axis_index("col")
    nz = lax.axis_size("z")
    depth, width = child_factor.shape
    k = depth * nz * NB
    zh = nz // 2
    sub = width // (zh * NB)
    hs = sub // 2
    tiles_dev = root_cov.shape[0] // BLK
    col_tiles = root_cov.shape[1] // BLK
    kb = structure.shape[0]
    picked = select_columns(root_cov, structure - c * col_tiles)
    half = lax.psum_scatter(picked, "col", scatter_dimension=1, tiled=True)
    first = (z * NB + b) * tiles_dev
    parts = []
    for j in range(2):
        at = structure[j] - first
        inside = (at >= 0) & (at < tiles_dev) & (c == 0)
        start = jnp.clip(at, 0, tiles_dev - 1) * BLK
        piece = lax.dynamic_slice(half, (start, 0), (BLK, 2 * BLK))
        parts.append(jnp.where(inside, piece, 0.0))
    low_low = lax.psum(jnp.concatenate(parts, axis=0), ("z", "b", "col"))
    f_b = child_factor.reshape(depth, zh, NB, sub).transpose(2, 0, 1, 3).reshape(NB, depth, zh * sub)
    f_i, f_j, s, slo = gather_blocks(f_b, half.reshape(tiles_dev, BLK, half.shape[1]))
    f_i = f_i.reshape(k, zh * sub)
    f_j = f_j.reshape(k, NB * hs)
    rows = s.reshape(2 * tiles_dev, BLK, k)
    place = (structure // 3) % NB * 6 + (structure // 12 - 2) * 3 + structure % 3
    low_own = s[..., : 2 * BLK]
    low_all = jnp.where((lax.iota(jnp.int32, NB) == b)[:, None, None, None, None], low_own[None], slo)
    col = jnp.minimum(b, 1) * BLK
    low_all = lax.dynamic_slice_in_dim(low_all.reshape(NB * 6, BLK, 2 * BLK), col, BLK, axis=2)
    low_row = jnp.take(low_all, place[2:], axis=0, mode="clip").reshape((kb - 2) * BLK, BLK).T
    low_row = jnp.concatenate([lax.dynamic_slice(low_low, (col, 0), (BLK, 2 * BLK)), low_row], axis=1)
    spare = jnp.where(b < 2, low_row, rows[0])
    rows = lax.dynamic_update_slice(rows, spare[None], (0, 0, 0)).reshape(6 * BLK, k)
    x = -jnp.dot(rows, f_j, precision=HIGH, preferred_element_type=jnp.float32)
    x_all = lax.all_gather(x, "b", axis=0, tiled=True).reshape(NB * 6, BLK, NB * hs)
    place = jnp.concatenate([jnp.array([0, 6], jnp.int32), place[2:]])
    x_all = permute_tiles(x_all, place)
    x3 = lax.dynamic_slice_in_dim(x_all.reshape(nz, NB, depth, NB * hs), b, 1, axis=1)[:, 0]
    x_all = lax.all_gather(x_all.reshape(k, NB * hs), "col", axis=0, tiled=False)
    out = lax.dot_general(
        x_all, f_i, (((1,), (0,)), ((), ())), precision=HIGH,
        preferred_element_type=jnp.float32,
    )
    child, cross_cov = scatter_blocks(out.reshape(2, NB, hs, zh * sub), x3)
    return (cross_cov, child_diag - child.reshape(2 * hs, width))


def solution(mesh):
    rows, cols = mesh.shape["row"], mesh.shape["col"]
    if cols == 2 and rows == 4 * NB:
        split = Mesh(mesh.devices.reshape(rows // NB, NB, cols), ("z", "b", "col"))
        spec = P(("z", "b"), "col")
        return jax.shard_map(
            grouped_device, mesh=split, in_specs=(spec, P(), spec, spec),
            out_specs=(spec, spec), check_vma=False,
        )
    spec = P("row", "col")
    return jax.shard_map(
        plain_device, mesh=mesh, in_specs=(spec, P(), spec, spec),
        out_specs=(spec, spec), check_vma=False,
    )
```
